512 devices in a mesh: row: 16 (over x, y_hi, core), col: 32 (over y_lo, z).
Axes of the slice: x: 4, y: 4 (y_hi: 2, y_lo: 2; y = y_hi * 2 + y_lo), z: 16, core: 2. Of those that a mesh axis runs over, the one named last changes fastest.
Arguments:
- pair: bfloat16 [640, 640, 128], P('row', 'col'), may hold values from -6 to 6
- norm_gain: float32 [128], replicated, may hold values from 0.1 to 1.9
- proj_weight: bfloat16 [128, 512], replicated, may hold values from -0.5 to 0.5
- gate_weight: bfloat16 [128, 128], replicated, may hold values from -0.5 to 0.5
- out_gain: float32 [128], replicated, may hold values from 0.1 to 1.9
- out_weight: bfloat16 [128, 128], replicated, may hold values from -0.5 to 0.5
Outputs:
- updated: bfloat16 [640, 640, 128], P('row', 'col')
The draws below stay inside these ranges and needn't reach their ends.
All inputs are finite; a program needn't handle non-finite values.
Results may differ from the reference program's by a relative error of at most 0.0054.
Values may be sent and summed in bfloat16 or wider, within the bound.
A program may use at most 128 MiB of HBM per device.

```python
import jax
import jax.numpy as jnp
from jax import lax

CZ = 128
CH = 128
RES = 640


def levels(rng, extent, cuts, smallest, largest):
    def one(position, blocks):
        steps = jax.random.uniform(jax.random.fold_in(jax.random.fold_in(rng, 6), position), (blocks,), jnp.float32, smallest / len(cuts), largest / len(cuts))
        return jnp.repeat(jnp.exp(steps), extent[position] // blocks).reshape((-1,) + (1,) * (len(extent) - position - 1))

    loudness = one(*cuts[0])
    for cut in cuts[1:]:
        loudness = loudness * one(*cut)
    return loudness


def gaussian(stream_key, extent, scale, most, split=(), dtype=jnp.bfloat16):
    level = levels(stream_key, extent, split, -0.22, 0.18) if split else 1.0
    result = jax.random.normal(stream_key, extent, jnp.float32) * scale * level
    return jnp.minimum(jnp.maximum(result, -most), most).astype(dtype)


def setup_inputs(seed: int = 0) -> dict:
    seeds = jax.random.split(jax.random.key(seed), 7)
    pair = gaussian(seeds[0], (RES, RES, CZ), 1.0, 6.0, ((0, 16), (1, 32)))
    norm_gain = jnp.clip(1.0 + 0.18 * jax.random.normal(seeds[1], (CZ,), jnp.float32), 0.1, 1.9)
    proj_weight = gaussian(seeds[2], (CZ, 4 * CH), CZ ** -0.5, 0.5)
    gate_weight = gaussian(seeds[3], (CZ, CZ), CZ ** -0.5, 0.5)
    out_gain = jnp.clip(1.0 + 0.18 * jax.random.normal(seeds[4], (CH,), jnp.float32), 0.1, 1.9)
    out_weight = gaussian(seeds[5], (CH, CZ), CH ** -0.5, 0.5)
    return dict(pair=pair, norm_gain=norm_gain, proj_weight=proj_weight, gate_weight=gate_weight, out_gain=out_gain, out_weight=out_weight)


epsilon = 1e-05

def layer_norm(values, weights):
    center = lax.optimization_barrier(jnp.mean(values, axis=-1, keepdims=True))
    shifted = values - center
    spread = lax.optimization_barrier(jnp.mean(shifted * shifted, axis=-1, keepdims=True))
    return shifted * lax.rsqrt(spread + epsilon) * weights

def reference(pair, norm_gain, proj_weight, gate_weight, out_gain, out_weight):
    widened = pair.astype(jnp.float32)
    normed = layer_norm(widened, norm_gain).astype(jnp.bfloat16)
    flat_normed = normed.reshape(RES * RES, CZ)
    projected = jnp.dot(flat_normed, proj_weight, preferred_element_type=jnp.float32).reshape(RES, RES, 4 * CH)
    left_factor = (jax.nn.sigmoid(projected[..., 0:CH]) * projected[..., CH:2 * CH]).astype(jnp.bfloat16)
    right_factor = (jax.nn.sigmoid(projected[..., 2 * CH:3 * CH]) * projected[..., 3 * CH:]).astype(jnp.bfloat16)
    gating = jax.nn.sigmoid(jnp.dot(flat_normed, gate_weight, preferred_element_type=jnp.float32)).reshape(RES, RES, CZ)
    summed = jnp.einsum('ikc,jkc->ijc', left_factor.astype(jnp.float32), right_factor.astype(jnp.float32), precision=lax.Precision.HIGHEST)
    mixed_low = layer_norm(summed, out_gain).astype(jnp.bfloat16)
    update = jnp.dot(mixed_low.reshape(RES * RES, CH), out_weight, preferred_element_type=jnp.float32).reshape(RES, RES, CZ)
    return (widened + gating * update).astype(jnp.bfloat16)
```

```python
import jax
import jax.numpy as jnp
from jax import lax
from jax.experimental import pallas as pl
from jax.experimental.pallas import tpu as pltpu
from jax.sharding import PartitionSpec as P

MESH = pl.DeviceIdType.MESH
F32 = jnp.float32
BF16 = jnp.bfloat16
EPS = 1e-05
NZ = 16
ROWS = 40
COLS = 20
PITCH = 24
NG = 7
CHUNKS = ((0, 2), (2, 2), (4, 2), (6, 1))
NCH = len(CHUNKS)
KROWS = 2 * 3 * NG * NZ


def lanes_of(shape):
    return lax.broadcasted_iota(jnp.int32, shape, 1)


def rows_of(shape):
    return lax.broadcasted_iota(jnp.int32, shape, 0)


def kernel(pair_ref, ngain_ref, proj_ref, gatew_ref, ogain_ref, outw_ref, out_ref,
           pf, nf, gat, wt, zs, zr, tb, ps, lb, rb, lt, rt_, st, tiles, sib, comb, back, xn, gcol, wf,
           zss, zrs, lss, lrs, rss, rrs, ess, ers, bss, brs):
    row = lax.axis_index("row")
    col = lax.axis_index("col")
    z, yl = col % NZ, col // NZ
    x1, x0, yh, core = row // 8, (row // 4) % 2, (row // 2) % 2, row % 2

    def dev(ax1, ax0, ayh, acore, ayl, az):
        return {"row": ax1 * 8 + ax0 * 4 + ayh * 2 + acore, "col": ayl * NZ + az}

    def left_target(n):
        return (x1, (x0 + n // 8) % 2, (yh + (n // 4) % 2) % 2, (core + (n // 2) % 2) % 2, (yl + n % 2) % 2)

    def right_target(n):
        return ((x1 + n // 8) % 2, (x0 + (n // 4) % 2) % 2, yh, (core + (n // 2) % 2) % 2, (yl + n % 2) % 2)

    barrier = pltpu.get_barrier_semaphore()

    def greet(t, az):
        pl.semaphore_signal(barrier, inc=1, device_id=dev(*t, az), device_id_type=MESH)

    @pl.loop(1, NZ)
    def _(d):
        greet((x1, x0, yh, core, yl), (z + d) % NZ)

    @pl.loop(1, 16)
    def _(n):
        greet(left_target(n), z)

    @pl.loop(8, 16)
    def _(n):
        greet(right_target(n), z)

    @pl.loop(0, ROWS)
    def _(i):
        base = pl.multiple_of(i * PITCH, 8)
        pf[pl.ds(base + 16, 8), :] = jnp.zeros((8, 128), F32)
        pf[pl.ds(base, COLS), :] = pair_ref[i].astype(F32)

    wt[...] = proj_ref[...].astype(F32).T.astype(BF16)
    ngain = ngain_ref[...]

    for g in range(NG):
        for s in range(3):
            v = pf[pl.ds(3 * g + s, ROWS, stride=PITCH), :]
            center = jnp.mean(v, axis=-1, keepdims=True)
            shifted = v - center
            spread = jnp.mean(shifted * shifted, axis=-1, keepdims=True)
            nf[128 * g + 40 * s : 128 * g + 40 * s + 40, :] = shifted * lax.rsqrt(spread + EPS) * ngain
        nf[128 * g + 120 : 128 * g + 128, :] = jnp.zeros((8, 128), F32)

    nt = (((1,), (1,)), ((), ()))

    @pl.loop(0, NG)
    def _(g):
        n_g = nf[pl.ds(pl.multiple_of(g * 128, 128), 128), :].astype(BF16)
        p = lax.dot_general(wt[...], n_g, nt, preferred_element_type=F32)
        left = jax.nn.sigmoid(p[0:128]) * p[128:256]
        right = jax.nn.sigmoid(p[256:384]) * p[384:512]
        for t in range(NZ):
            zs[t, g] = jnp.concatenate([left[8 * t : 8 * t + 8], right[8 * t : 8 * t + 8]], axis=0).astype(BF16)

    pl.semaphore_wait(barrier, 15 + 15 + 8)

    def z_copy(ci, d):
        g0, n = CHUNKS[ci]
        t = (z + d) % NZ
        return pltpu.make_async_remote_copy(
            src_ref=zs.at[t, pl.ds(g0, n)], dst_ref=zr.at[z, pl.ds(g0, n)],
            send_sem=zss.at[ci, d], recv_sem=zrs.at[ci, d],
            device_id=dev(x1, x0, yh, core, yl, t), device_id_type=MESH)

    for ci in range(NCH):
        @pl.loop(0, 15)
        def _(k, ci=ci):
            d = 8 + (k + 1) // 2 * (1 - 2 * (k % 2))
            z_copy(ci, d).start()

    zr[z] = zs[z]

    @pl.loop(0, NG)
    def _(g):
        rows = pl.ds(pl.multiple_of(g * 128, 128), 128)
        gat[rows, :] = jax.nn.sigmoid(jnp.dot(nf[rows, :].astype(BF16), gatew_ref[...], preferred_element_type=F32))

    gcol[...] = jnp.broadcast_to(ogain_ref[...], (128, 128)).T
    wf[...] = outw_ref[...].astype(F32)

    def l_copy(ci, n):
        g0, m = CHUNKS[ci]
        t = left_target(n)
        return pltpu.make_async_remote_copy(
            src_ref=ps.at[t[1] * 4 + t[4] * 2 + t[3], pl.ds(g0, m)],
            dst_ref=lb.at[(x0 * 4 + yh * 2 + core) * 2 + yl, pl.ds(g0, m)],
            send_sem=lss.at[ci, n], recv_sem=lrs.at[ci, n], device_id=dev(*t, z), device_id_type=MESH)

    def r_copy(ci, n):
        g0, m = CHUNKS[ci]
        t = right_target(n)
        return pltpu.make_async_remote_copy(
            src_ref=ps.at[8 + t[1] * 4 + t[4] * 2 + t[3], pl.ds(g0, m)],
            dst_ref=rb.at[(x1 * 4 + x0 * 2 + core) * 2 + yl, pl.ds(g0, m)],
            send_sem=rss.at[ci, n], recv_sem=rrs.at[ci, n], device_id=dev(*t, z), device_id_type=MESH)

    channel = x0 * 4 + yl * 2 + core
    lane = lanes_of((NZ, 128))

    def regroup(src, dst, g):
        for y in range(2):
            for q in range(3):
                parts = [src[(3 * q + s) * 2 + y, g].astype(F32) for s in range(3 if q < 2 else 2)]
                for k in range(3):
                    moved = [pltpu.roll(v, (40 * (s - k)) % 128, 1) if s != k else v for s, v in enumerate(parts)]
                    tile = jnp.where(lane < 40, moved[0], moved[1])
                    if len(moved) > 2:
                        tile = jnp.where(lane < 80, tile, moved[2])
                    dst[pl.ds(pl.multiple_of(((y * NG + g) * 3 + k) * NZ, NZ), NZ), q * 128 : q * 128 + 128] = tile.astype(BF16)

    def plane_in(ci):
        g0, m = CHUNKS[ci]

        @pl.loop(1, 16)
        def _(n):
            l_copy(ci, n).wait_recv()
            r_copy(ci, n).wait_recv()

        @pl.loop(g0, g0 + m)
        def _(g):
            regroup(lb, lt, g)
            regroup(rb, rt_, g)

    for ci in range(NCH):
        g0, m = CHUNKS[ci]

        @pl.loop(1, NZ)
        def _(d, ci=ci):
            z_copy(ci, d).wait_recv()

        @pl.loop(g0, g0 + m)
        def _(g):
            for t in range(NZ):
                tb[16 * t : 16 * t + 16, :] = zr[t, g].astype(F32)
            for c in range(16):
                ps[c, g] = tb[pl.ds(c, NZ, stride=16), :].astype(BF16)

        @pl.loop(1, 16)
        def _(n, ci=ci):
            l_copy(ci, n).start()
            r_copy(ci, n).start()

        lb[(x0 * 4 + yh * 2 + core) * 2 + yl, pl.ds(g0, m)] = ps[channel, pl.ds(g0, m)]
        rb[(x1 * 4 + x0 * 2 + core) * 2 + yl, pl.ds(g0, m)] = ps[8 + channel, pl.ds(g0, m)]
        if ci > 0:
            plane_in(ci - 1)
    plane_in(NCH - 1)

    tn = (((0,), (0,)), ((), ()))
    st[...] = lax.dot_general(rt_[...], lt[...], tn, preferred_element_type=F32)

    for half in range(2):
        mine = half == core
        shift = jnp.where(mine, 0, 40)
        main = (lane >= shift) & (lane < shift + 40)
        erow = jnp.where(mine, 0, 8)
        rowi = rows_of((NZ, 128))
        extra = (lane >= 80) & (lane < 120) & (rowi >= erow) & (rowi < erow + 4)
        for jj in range(4):
            rj = 4 * half + jj
            for h in range(2):
                base = 128 * (rj // 3) + 40 * (rj % 3) + 20 * h
                for q in range(3):
                    a = st[base : base + 16, 128 * q : 128 * q + 128]
                    b = st[base + 16 : base + 24, 128 * q : 128 * q + 128]
                    b = jnp.concatenate([b, b], axis=0)
                    for s in range(3 if q < 2 else 2):
                        am = pltpu.roll(a, (shift - 40 * s + 128) % 128, 1)
                        bm = pltpu.roll(b, (80 - 40 * s) % 128, 1) if s != 2 else b
                        tile = jnp.where(main, am, jnp.where(extra, bm, 0.0))
                        tiles[half, (jj * 2 + h) * 8 + 3 * q + s] = tile.astype(BF16)

    swap = pltpu.make_async_remote_copy(
        src_ref=tiles.at[1 - core], dst_ref=sib, send_sem=ess, recv_sem=ers,
        device_id=dev(x1, x0, yh, 1 - core, yl, z), device_id_type=MESH)
    swap.start()
    swap.wait_recv()

    m_me = z * 4 + x0 * 2 + yl

    def b_target(n):
        j = (n // 8 + z) % 8
        i = (n + x0 * 4 + yh * 2 + core) % 8
        zt = 8 * (j // 4) + 4 * yh + 2 * ((j // 2) % 2) + j % 2
        same = (i == x0 * 4 + yh * 2 + core) & (core == yl) & (zt == z)
        return j * 8 + i, dev(x1, i // 4, (i // 2) % 2, i % 2, core, zt), same

    def b_copy(n):
        k, d, same = b_target(n)
        return same, k, pltpu.make_async_remote_copy(
            src_ref=comb.at[k], dst_ref=back.at[m_me], send_sem=bss, recv_sem=brs, device_id=d, device_id_type=MESH)

    @pl.loop(0, 64)
    def _(n):
        same, k, cp = b_copy(n)
        comb[k] = (tiles[core, k].astype(F32) + sib[k].astype(F32)).astype(BF16)

        @pl.when(jnp.logical_not(same))
        def _():
            cp.start()

        @pl.when(same)
        def _():
            pltpu.make_async_copy(comb.at[k], back.at[m_me], brs).start()

    pltpu.make_async_copy(comb, back, brs).wait()

    def total(step):
        def add(m, acc):
            for u in range(8):
                acc = acc + step(m * 8 + u)
            return acc
        s = lax.fori_loop(0, 8, add, jnp.zeros((NZ, 128), F32))
        both = s + pltpu.roll(s, 88, 1)
        e = s[0:8] + s[8:16]
        return jnp.where(lane < 40, both, jnp.where(lane < 80, pltpu.roll(both, 40, 1), jnp.concatenate([e, e], axis=0))) * (1.0 / 128.0)

    mean = total(lambda m: back[m].astype(F32))

    def square(m):
        d = back[m].astype(F32) - mean
        return d * d
    scale = lax.rsqrt(total(square) + EPS)

    @pl.loop(0, 64)
    def _(m):
        xn[pl.ds(pl.multiple_of(m * 16, 16), 16), :] = (back[m].astype(F32) - mean) * scale

    even, odd = gcol[pl.ds(0, 64, stride=2), :], gcol[pl.ds(1, 64, stride=2), :]
    g_a, g_b = jnp.where(yl == 0, even, odd), jnp.where(yl == 0, odd, even)
    even, odd = wf[pl.ds(0, 64, stride=2), :], wf[pl.ds(1, 64, stride=2), :]
    w_ab = jnp.concatenate([jnp.where(yl == 0, even, odd), jnp.where(yl == 0, odd, even)], axis=1).astype(BF16)
    lane64 = lanes_of((64, 128))
    rest = {}
    for t in range(16):
        gain = jnp.where(lane64 < 40, g_a, jnp.where(lane64 < 80, g_b, g_a if t < 8 else g_b))
        x = (xn[pl.ds(t, 64, stride=16), :] * gain).astype(BF16)
        y = lax.dot_general(x, w_ab, tn, preferred_element_type=F32)
        done = [(t, y[0:40, 0:128] + y[40:80, 128:256])]
        if t < 4:
            rest[t] = y[80:120, 0:128]
        if 8 <= t < 12:
            done.append((t + 8, rest[t - 8] + y[80:120, 128:256]))
        for k, u in done:
            at = 128 * (k // 3) + 40 * (k % 3)
            pf[pl.ds(k, ROWS, stride=PITCH), :] = pf[pl.ds(k, ROWS, stride=PITCH), :] + gat[at : at + 40, :] * u

    @pl.loop(0, ROWS)
    def _(i):
        out_ref[i] = pf[pl.ds(pl.multiple_of(i * PITCH, 8), COLS), :].astype(BF16)

    for ci in range(NCH):
        @pl.loop(1, 16)
        def _(n, ci=ci):
            z_copy(ci, n).wait_send()
            l_copy(ci, n).wait_send()
            r_copy(ci, n).wait_send()
    swap.wait_send()

    @pl.loop(0, 64)
    def _(n):
        same, k, cp = b_copy(n)

        @pl.when(jnp.logical_not(same))
        def _():
            cp.wait_send()


def shards(pair, norm_gain, proj_weight, gate_weight, out_gain, out_weight):
    vm = pl.BlockSpec(memory_space=pltpu.VMEM)
    dma = pltpu.SemaphoreType.DMA
    return pl.pallas_call(
        kernel,
        out_shape=jax.ShapeDtypeStruct(pair.shape, BF16),
        in_specs=[vm] * 6,
        out_specs=vm,
        scratch_shapes=[
            pltpu.VMEM((ROWS * PITCH, 128), F32),
            pltpu.VMEM((NG * 128, 128), F32),
            pltpu.VMEM((NG * 128, 128), F32),
            pltpu.VMEM((512, 128), BF16),
            pltpu.VMEM((NZ, NG, 16, 128), BF16),
            pltpu.VMEM((NZ, NG, 16, 128), BF16),
            pltpu.VMEM((256, 128), F32),
            pltpu.VMEM((16, NG, 16, 128), BF16),
            pltpu.VMEM((16, NG, 16, 128), BF16),
            pltpu.VMEM((16, NG, 16, 128), BF16),
            pltpu.VMEM((KROWS, 384), BF16),
            pltpu.VMEM((KROWS, 384), BF16),
            pltpu.VMEM((384, 384), F32),
            pltpu.VMEM((2, 64, 16, 128), BF16),
            pltpu.VMEM((64, 16, 128), BF16),
            pltpu.VMEM((64, 16, 128), BF16),
            pltpu.VMEM((64, 16, 128), BF16),
            pltpu.VMEM((1024, 128), F32),
            pltpu.VMEM((128, 128), F32),
            pltpu.VMEM((128, 128), F32),
            dma((NCH, 16)), dma((NCH, 16)),
            dma((NCH, 16)), dma((NCH, 16)),
            dma((NCH, 16)), dma((NCH, 16)),
            dma, dma, dma, dma,
        ],
        compiler_params=pltpu.CompilerParams(collective_id=0, has_side_effects=True, vmem_limit_bytes=40 * 1024 * 1024),
        name="triangle",
    )(pair, norm_gain.reshape(1, -1), proj_weight, gate_weight, out_gain.reshape(1, -1), out_weight)


def solution(mesh):
    in_specs = (P("row", "col", None), P(), P(), P(), P(), P())
    return jax.shard_map(shards, mesh=mesh, in_specs=in_specs, out_specs=P("row", "col", None), check_vma=False)
```

```python
import jax
import jax.numpy as jnp
from jax import lax
from jax.experimental import pallas as pl
from jax.experimental.pallas import tpu as pltpu
from jax.sharding import PartitionSpec as P

MESH = pl.DeviceIdType.MESH
F32 = jnp.float32
BF16 = jnp.bfloat16
EPS = 1e-05
NZ = 16
ROWS = 40
COLS = 20
NG = 7
CHUNKS = ((0, 4), (4, 3))
NCH = len(CHUNKS)
KROWS = 2 * 3 * NG * NZ
NL = 4
BACK = ((0, 1), (1, 3))
NBC = len(BACK)


def lanes_of(shape):
    return lax.broadcasted_iota(jnp.int32, shape, 1)


def rows_of(shape):
    return lax.broadcasted_iota(jnp.int32, shape, 0)


def kernel(pair_in, ngain_in, proj_in, gatew_in, ogain_in, outw_in, out_ref,
           pair_ref, ngain_ref, proj_ref, gatew_ref, ogain_ref, outw_ref, nf, gat, wt, zs, zr, tb, ps, lb, rb, lt, rt_, total, st, tiles, back, zb, zo, gcol,
           zss, zrs, lss, lrs, rss, rrs, ess, ers, bss, brs, ins):
    row = lax.axis_index("row")
    col = lax.axis_index("col")
    z, yl = col % NZ, col // NZ
    x1, x0, yh, core = row // 8, (row // 4) % 2, (row // 2) % 2, row % 2

    flips = {"x1": (8 * (1 - 2 * x1), 0, 0), "x0": (4 * (1 - 2 * x0), 0, 4 * (1 - 2 * x0)), "yh": (2 * (1 - 2 * yh), 0, 0),
             "core": (1 - 2 * core, 0, 1 - 2 * core), "yl": (0, NZ * (1 - 2 * yl), 2 * (1 - 2 * yl))}
    channel = x0 * 4 + yl * 2 + core

    def flipped(names):
        r, c, k = row, col, channel
        for name in names:
            r, c, k = r + flips[name][0], c + flips[name][1], k + flips[name][2]
        return {"row": r, "col": c}, k

    def subsets(names):
        found = [[n for i, n in enumerate(names) if m >> i & 1] for m in range(1, 16)]
        return sorted(found, key=lambda f: -len(f))

    left_partners = subsets(("x0", "yh", "yl", "core"))
    right_partners = subsets(("x1", "x0", "yl", "core"))
    far_first = [8] + [d for k in range(7, 0, -1) for d in (k, NZ - k)]

    def along(d):
        t = lax.rem(z + d, NZ)
        return t, {"row": row, "col": yl * NZ + t}

    def remote(src, dst, send_sem, recv_sem, to):
        pltpu.make_async_remote_copy(
            src_ref=src, dst_ref=dst, send_sem=send_sem, recv_sem=recv_sem, device_id=to, device_id_type=MESH).start()

    def all_of(ref, sem):
        pltpu.make_async_copy(ref, ref, sem).wait()

    ins_from = (pair_in, proj_in, ngain_in, gatew_in, ogain_in, outw_in)
    ins_to = (pair_ref, proj_ref, ngain_ref, gatew_ref, ogain_ref, outw_ref)
    fetch = [pltpu.make_async_copy(a, b, ins.at[n]) for n, (a, b) in enumerate(zip(ins_from, ins_to))]
    for f in fetch:
        f.start()

    barrier = pltpu.get_barrier_semaphore()
    greeted = [along(d)[1] for d in far_first]
    greeted += [flipped(f)[0] for f in left_partners] + [flipped(f)[0] for f in right_partners if "x1" in f]
    for to in greeted:
        pl.semaphore_signal(barrier, inc=1, device_id=to, device_id_type=MESH)

    for f in fetch:
        f.wait()
    wt[...] = proj_ref[...].astype(F32).T.astype(BF16)
    ngain = ngain_ref[...]

    for g in range(NG):
        for s in range(3):
            at = 128 * g + 40 * s
            if 3 * g + s < COLS:
                v = pair_ref[3 * g + s].astype(F32)
                center = jnp.mean(v, axis=-1, keepdims=True)
                shifted = v - center
                spread = jnp.mean(shifted * shifted, axis=-1, keepdims=True)
                nf[at : at + 40, :] = shifted * lax.rsqrt(spread + EPS) * ngain
            else:
                nf[at : at + 40, :] = jnp.zeros((40, 128), F32)
        nf[128 * g + 120 : 128 * g + 128, :] = jnp.zeros((8, 128), F32)

    nt = (((1,), (1,)), ((), ()))

    @pl.loop(0, NG)
    def _(g):
        n_g = nf[pl.ds(pl.multiple_of(g * 128, 128), 128), :].astype(BF16)
        p = lax.dot_general(wt[...], n_g, nt, preferred_element_type=F32)
        left = jax.nn.sigmoid(p[0:128]) * p[128:256]
        right = jax.nn.sigmoid(p[256:384]) * p[384:512]
        for t in range(NZ):
            zs[t, g] = jnp.concatenate([left[8 * t : 8 * t + 8], right[8 * t : 8 * t + 8]], axis=0).astype(BF16)

    pl.semaphore_wait(barrier, len(greeted))

    for ci, (g0, m) in enumerate(CHUNKS):
        for d in far_first:
            t, to = along(d)
            remote(zs.at[t, pl.ds(g0, m)], zr.at[z, pl.ds(g0, m)], zss.at[ci], zrs.at[ci], to)

    zr[z] = zs[z]

    @pl.loop(0, NG)
    def _(g):
        rows = pl.ds(pl.multiple_of(g * 128, 128), 128)
        gat[rows, :] = jax.nn.sigmoid(jnp.dot(nf[rows, :].astype(BF16), gatew_ref[...], preferred_element_type=F32))

    gcol[...] = jnp.broadcast_to(ogain_ref[...], (128, 128)).T

    lane = lanes_of((NZ, 128))

    def regroup(src, dst, g):
        for y in range(2):
            for q in range(3):
                parts = [src[(3 * q + s) * 2 + y, g].astype(F32) for s in range(3 if q < 2 else 2)]
                for k in range(3):
                    moved = [pltpu.roll(v, (40 * (s - k)) % 128, 1) if s != k else v for s, v in enumerate(parts)]
                    tile = jnp.where(lane < 40, moved[0], moved[1])
                    if len(moved) > 2:
                        tile = jnp.where(lane < 80, tile, moved[2])
                    dst[pl.ds(pl.multiple_of(((g * 2 + y) * 3 + k) * NZ, NZ), NZ), q * 128 : q * 128 + 128] = tile.astype(BF16)

    tn = (((0,), (0,)), ((), ()))
    l_me, r_me = (x0 * 4 + yh * 2 + core) * 2 + yl, (x1 * 4 + x0 * 2 + core) * 2 + yl

    def plane_in(ci):
        g0, m = CHUNKS[ci]
        for src, dst, sem in ((lb, lt, lrs.at[ci]), (rb, rt_, rrs.at[ci])):
            all_of(src.at[pl.ds(0, 15), pl.ds(g0, m)], sem)

            @pl.loop(g0, g0 + m)
            def _(g, src=src, dst=dst):
                regroup(src, dst, g)
        rows = pl.ds(g0 * 96, m * 96)
        return lax.dot_general(rt_[rows, :], lt[rows, :], tn, preferred_element_type=F32)

    for ci, (g0, m) in enumerate(CHUNKS):
        all_of(zr.at[pl.ds(0, 15), pl.ds(g0, m)], zrs.at[ci])

        @pl.loop(g0, g0 + m)
        def _(g):
            for t in range(NZ):
                tb[16 * t : 16 * t + 16, :] = zr[t, g].astype(F32)
            for c in range(16):
                ps[c, g] = tb[pl.ds(c, NZ, stride=16), :].astype(BF16)

        for f, h in zip(left_partners, right_partners):
            to, c = flipped(f)
            remote(ps.at[c, pl.ds(g0, m)], lb.at[l_me, pl.ds(g0, m)], lss.at[ci], lrs.at[ci], to)
            to, c = flipped(h)
            remote(ps.at[8 + c, pl.ds(g0, m)], rb.at[r_me, pl.ds(g0, m)], rss.at[ci], rrs.at[ci], to)

        lb[l_me, pl.ds(g0, m)] = ps[channel, pl.ds(g0, m)]
        rb[r_me, pl.ds(g0, m)] = ps[8 + channel, pl.ds(g0, m)]
        if ci > 0:
            part = plane_in(ci - 1)
            total[...] = part if ci == 1 else total[...] + part
    s_t = plane_in(NCH - 1)
    if NCH > 1:
        s_t = s_t + total[...]
    for r in range(8):
        at = 128 * (r // 3) + 40 * (r % 3)
        for q in range(3):
            st[q * 320 + r * 40 : q * 320 + r * 40 + 40, :] = s_t[at : at + 40, 128 * q : 128 * q + 128]

    lane8 = lanes_of((8, 128))

    for ci in range(NBC):
        l0, m = BACK[ci]
        for y in range(2):
            for l in range(l0, l0 + m):
                for q in range(3):
                    out = []
                    for h in range(2):
                        parts = [st[pl.ds(q * 320 + 160 * y + 10 * h + 3 * l + k, 8, stride=20), :] for k in range(3 if l < 3 else 1)]
                        per = []
                        for r in range(3 if q < 2 else 2):
                            moved = [pltpu.roll(v, (40 * (k - r)) % 128, 1) if k != r else v for k, v in enumerate(parts)]
                            moved += [jnp.zeros((8, 128), F32)] * (3 - len(moved))
                            per.append(jnp.where(lane8 < 40, moved[0], jnp.where(lane8 < 80, moved[1], moved[2])))
                        out.append(per)
                    for r in range(len(out[0])):
                        tiles[(3 * q + r) * 2 + y, l] = jnp.concatenate([out[0][r], out[1][r]], axis=0).astype(BF16)

        for f in left_partners:
            to, _ = flipped(f)
            owner = l_me + 2 * sum(flips[n][0] for n in f if n != "yl") + (1 - 2 * yl if "yl" in f else 0)
            remote(tiles.at[owner, pl.ds(l0, m)], back.at[channel * 2 + yh, pl.ds(l0, m)], ess.at[ci], ers.at[ci], to)
        back[channel * 2 + yh, pl.ds(l0, m)] = tiles[l_me, pl.ds(l0, m)]

    for ci, (l0, m) in enumerate(BACK):
        all_of(back.at[pl.ds(0, 15), pl.ds(l0, m)], ers.at[ci])

        @pl.loop(l0, l0 + m)
        def _(l):
            for h in range(2):
                for c in range(8):
                    tb[16 * c : 16 * c + 16, :] = back[c * 2 + h, l].astype(F32)
                for k in range(8):
                    rows = [tb[pl.ds(8 * u + k, 8, stride=16), :] for u in range(2)]
                    zb[8 * (k // 4) + 4 * h + k % 4, l] = jnp.concatenate(rows, axis=0).astype(BF16)

        for d in far_first:
            t, to = along(d)
            remote(zb.at[t, pl.ds(l0, m)], zo.at[z, pl.ds(l0, m)], bss.at[ci], brs.at[ci], to)
        zo[z, pl.ds(l0, m)] = zb[z, pl.ds(l0, m)]

    for l in range(NL):
        for ci, (l0, m) in enumerate(BACK):
            if l == l0:
                all_of(zo.at[pl.ds(0, 15), pl.ds(l0, m)], brs.at[ci])
        for h in range(2):
            v = jnp.concatenate([zo[t, l].astype(F32)[8 * h : 8 * h + 8] for t in range(NZ)], axis=0)
            center = jnp.mean(v, axis=0, keepdims=True)
            shifted = v - center
            spread = jnp.mean(shifted * shifted, axis=0, keepdims=True)
            x = (shifted * lax.rsqrt(spread + EPS) * gcol[...]).astype(BF16)
            u = lax.dot_general(x, outw_ref[...], tn, preferred_element_type=F32)
            for k in range(3 if l < 3 else 1):
                j = 10 * h + 3 * l + k
                at = 128 * (j // 3) + 40 * (j % 3)
                out_ref[j] = (pair_ref[j].astype(F32) + gat[at : at + 40, :] * u[40 * k : 40 * k + 40]).astype(BF16)

    for ci, (g0, m) in enumerate(CHUNKS):
        for ref, sem in ((zs, zss), (ps, lss), (ps, rss)):
            all_of(ref.at[pl.ds(0, 15), pl.ds(g0, m)], sem.at[ci])
    for ci, (l0, m) in enumerate(BACK):
        for ref, sem in ((tiles, ess), (zb, bss)):
            all_of(ref.at[pl.ds(0, 15), pl.ds(l0, m)], sem.at[ci])


def shards(pair, norm_gain, proj_weight, gate_weight, out_gain, out_weight):
    vm = pl.BlockSpec(memory_space=pltpu.VMEM)
    dma = pltpu.SemaphoreType.DMA
    out = pl.pallas_call(
        kernel,
        out_shape=jax.ShapeDtypeStruct((COLS, ROWS, 128), BF16),
        in_specs=[pl.BlockSpec(memory_space=pl.ANY)] * 6,
        out_specs=vm,
        scratch_shapes=[
            pltpu.VMEM((COLS, ROWS, 128), BF16),
            pltpu.VMEM((1, 128), F32),
            pltpu.VMEM((128, 512), BF16),
            pltpu.VMEM((128, 128), BF16),
            pltpu.VMEM((1, 128), F32),
            pltpu.VMEM((128, 128), BF16),
            pltpu.VMEM((NG * 128, 128), F32),
            pltpu.VMEM((NG * 128, 128), F32),
            pltpu.VMEM((512, 128), BF16),
            pltpu.VMEM((NZ, NG, 16, 128), BF16),
            pltpu.VMEM((NZ, NG, 16, 128), BF16),
            pltpu.VMEM((256, 128), F32),
            pltpu.VMEM((16, NG, 16, 128), BF16),
            pltpu.VMEM((16, NG, 16, 128), BF16),
            pltpu.VMEM((16, NG, 16, 128), BF16),
            pltpu.VMEM((KROWS, 384), BF16),
            pltpu.VMEM((KROWS, 384), BF16),
            pltpu.VMEM((384, 384), F32),
            pltpu.VMEM((960, 128), F32),
            pltpu.VMEM((16, NL, 16, 128), BF16),
            pltpu.VMEM((16, NL, 16, 128), BF16),
            pltpu.VMEM((NZ, NL, 16, 128), BF16),
            pltpu.VMEM((NZ, NL, 16, 128), BF16),
            pltpu.VMEM((128, 128), F32),
            dma((NCH,)), dma((NCH,)), dma((NCH,)), dma((NCH,)), dma((NCH,)), dma((NCH,)),
            dma((NBC,)), dma((NBC,)), dma((NBC,)), dma((NBC,)), dma((6,)),
        ],
        compiler_params=pltpu.CompilerParams(collective_id=0, has_side_effects=True, vmem_limit_bytes=63 * 1024 * 1024),
        name="triangle",
    )(jnp.transpose(pair, (1, 0, 2)), norm_gain.reshape(1, -1), proj_weight, gate_weight, out_gain.reshape(1, -1), out_weight)
    return jnp.transpose(out, (1, 0, 2))


def solution(mesh):
    in_specs = (P("row", "col", None), P(), P(), P(), P(), P())
    return jax.shard_map(shards, mesh=mesh, in_specs=in_specs, out_specs=P("row", "col", None), check_vma=False)
```

```python
import jax
import jax.numpy as jnp
from jax import lax
from jax.experimental import pallas as pl
from jax.experimental.pallas import tpu as pltpu
from jax.sharding import PartitionSpec as P

MESH = pl.DeviceIdType.MESH
F32 = jnp.float32
BF16 = jnp.bfloat16
EPS = 1e-05
NZ = 16
ROWS = 40
COLS = 20
NG = 7
CHUNKS = ((0, 4), (4, 3))
NCH = len(CHUNKS)
KROWS = 2 * 3 * NG * NZ
NL = 4
BACK = ((0, 1), (1, 3))
NBC = len(BACK)


def lanes_of(shape):
    return lax.broadcasted_iota(jnp.int32, shape, 1)


def rows_of(shape):
    return lax.broadcasted_iota(jnp.int32, shape, 0)


def kernel(pair_in, ngain_in, proj_in, gatew_in, ogain_in, outw_in, out_ref,
           pair_ref, ngain_ref, proj_ref, gatew_ref, ogain_ref, outw_ref, nf, gat, wt, zs, zr, tb, ps, lb, rb, lt, rt_, total, st, tiles, back, zb, zo, gcol,
           zss, zrs, lss, lrs, rss, rrs, fss, frs, ess, ers, bss, brs, ins):
    row = lax.axis_index("row")
    col = lax.axis_index("col")
    z, yl = col % NZ, col // NZ
    x1, x0, yh, core = row // 8, (row // 4) % 2, (row // 2) % 2, row % 2

    fx1, fx0, fyh, fyl = 1 - 2 * x1, 1 - 2 * x0, 1 - 2 * yh, 1 - 2 * yl
    flips = {"x1": (8 * fx1, 0, 4 * fx1, 8 * fx1), "x0": (4 * fx0, 0, 2 * fx0, 4 * fx0),
             "yh": (2 * fyh, 0, 0, 2 * fyh), "yl": (0, NZ * fyl, fyl, fyl)}
    channel = x1 * 4 + x0 * 2 + yl
    place = (x1 * 4 + x0 * 2 + yh) * 2 + yl
    r_place = core * 8 + (x1 * 2 + x0) * 2 + yl
    sibling = {"row": row + 1 - 2 * core, "col": col}

    def flipped(names):
        r, c, k, p = row, col, channel, place
        for name in names:
            r, c, k, p = r + flips[name][0], c + flips[name][1], k + flips[name][2], p + flips[name][3]
        return {"row": r, "col": c}, k, p

    def subsets(names):
        found = [[n for i, n in enumerate(names) if m >> i & 1] for m in range(1, 2 ** len(names))]
        return sorted(found, key=lambda f: -len(f))

    left_partners = subsets(("x1", "x0", "yh", "yl"))
    right_partners = subsets(("x1", "x0", "yl"))
    far_first = [8] + [d for k in range(7, 0, -1) for d in (k, NZ - k)]

    def along(d):
        t = lax.rem(z + d, NZ)
        return t, {"row": row, "col": yl * NZ + t}

    def remote(src, dst, send_sem, recv_sem, to):
        pltpu.make_async_remote_copy(
            src_ref=src, dst_ref=dst, send_sem=send_sem, recv_sem=recv_sem, device_id=to, device_id_type=MESH).start()

    def all_of(ref, sem):
        pltpu.make_async_copy(ref, ref, sem).wait()

    ins_from = (pair_in, proj_in, ngain_in, gatew_in, ogain_in, outw_in)
    ins_to = (pair_ref, proj_ref, ngain_ref, gatew_ref, ogain_ref, outw_ref)
    fetch = [pltpu.make_async_copy(a, b, ins.at[n]) for n, (a, b) in enumerate(zip(ins_from, ins_to))]
    for f in fetch:
        f.start()

    barrier = pltpu.get_barrier_semaphore()
    greeted = [along(d)[1] for d in far_first]
    greeted += [flipped(f)[0] for f in left_partners] + [sibling]
    for to in greeted:
        pl.semaphore_signal(barrier, inc=1, device_id=to, device_id_type=MESH)

    nt = (((1,), (1,)), ((), ()))
    for ci, (g0, m) in enumerate(CHUNKS):
        if ci == 0:
            fetch[0].wait()
            fetch[2].wait()
        ngain = ngain_ref[...]
        for g in range(g0, g0 + m):
            for s in range(3):
                at = 128 * g + 40 * s
                if 3 * g + s < COLS:
                    v = pair_ref[3 * g + s].astype(F32)
                    center = jnp.mean(v, axis=-1, keepdims=True)
                    shifted = v - center
                    spread = jnp.mean(shifted * shifted, axis=-1, keepdims=True)
                    nf[at : at + 40, :] = shifted * lax.rsqrt(spread + EPS) * ngain
                else:
                    nf[at : at + 40, :] = jnp.zeros((40, 128), F32)
            nf[128 * g + 120 : 128 * g + 128, :] = jnp.zeros((8, 128), F32)
        if ci == 0:
            fetch[1].wait()
            wt[...] = proj_ref[...].astype(F32).T.astype(BF16)

        @pl.loop(g0, g0 + m)
        def _(g):
            n_g = nf[pl.ds(pl.multiple_of(g * 128, 128), 128), :].astype(BF16)
            p = lax.dot_general(wt[...], n_g, nt, preferred_element_type=F32)
            left = jax.nn.sigmoid(p[0:128]) * p[128:256]
            right = jax.nn.sigmoid(p[256:384]) * p[384:512]
            for t in range(NZ):
                zs[t, g] = jnp.concatenate([left[8 * t : 8 * t + 8], right[8 * t : 8 * t + 8]], axis=0).astype(BF16)

        if ci == 0:
            pl.semaphore_wait(barrier, len(greeted))

        for d in far_first:
            t, to = along(d)
            remote(zs.at[t, pl.ds(g0, m)], zr.at[z, pl.ds(g0, m)], zss.at[ci], zrs.at[ci], to)

    zr[z] = zs[z]

    for n in (3, 4, 5):
        fetch[n].wait()
    @pl.loop(0, NG)
    def _(g):
        rows = pl.ds(pl.multiple_of(g * 128, 128), 128)
        gat[rows, :] = jax.nn.sigmoid(jnp.dot(nf[rows, :].astype(BF16), gatew_ref[...], preferred_element_type=F32))

    gcol[...] = jnp.broadcast_to(ogain_ref[...], (128, 128)).T

    lane = lanes_of((NZ, 128))

    def regroup(src, dst, g, at):
        for y in range(2):
            for q in range(3):
                parts = [src[at(3 * q + s) + y, g].astype(F32) for s in range(3 if q < 2 else 2)]
                for k in range(3):
                    moved = [pltpu.roll(v, (40 * (s - k)) % 128, 1) if s != k else v for s, v in enumerate(parts)]
                    tile = jnp.where(lane < 40, moved[0], moved[1])
                    if len(moved) > 2:
                        tile = jnp.where(lane < 80, tile, moved[2])
                    dst[pl.ds(pl.multiple_of(((g * 2 + y) * 3 + k) * NZ, NZ), NZ), q * 128 : q * 128 + 128] = tile.astype(BF16)

    tn = (((0,), (0,)), ((), ()))

    def plane_in(ci):
        g0, m = CHUNKS[ci]
        all_of(rb.at[pl.ds(0, 7), pl.ds(g0, m)], rrs.at[ci])
        mine = rb.at[pl.ds(8 * core, 8), pl.ds(g0, m)]
        remote(mine, mine, fss.at[ci], frs.at[ci], sibling)
        all_of(lb.at[pl.ds(0, 15), pl.ds(g0, m)], lrs.at[ci])

        @pl.loop(g0, g0 + m)
        def _(g):
            regroup(lb, lt, g, lambda i: 2 * i)

        all_of(rb.at[pl.ds(0, 8), pl.ds(g0, m)], frs.at[ci])

        @pl.loop(g0, g0 + m)
        def _(g):
            regroup(rb, rt_, g, lambda j: 8 * (j % 2) + 2 * (j // 2))

        rows = pl.ds(g0 * 96, m * 96)
        return lax.dot_general(rt_[rows, :], lt[rows, :], tn, preferred_element_type=F32)

    for ci, (g0, m) in enumerate(CHUNKS):
        all_of(zr.at[pl.ds(0, 15), pl.ds(g0, m)], zrs.at[ci])

        @pl.loop(g0, g0 + m)
        def _(g):
            for t in range(NZ):
                tb[16 * t : 16 * t + 16, :] = zr[t, g].astype(F32)
            for c in range(16):
                ps[c, g] = tb[pl.ds(c, NZ, stride=16), :].astype(BF16)

        rb[r_place, pl.ds(g0, m)] = ps[8 + channel, pl.ds(g0, m)]
        lb[place, pl.ds(g0, m)] = ps[channel, pl.ds(g0, m)]
        for f in right_partners:
            to, c, _ = flipped(f)
            remote(ps.at[8 + c, pl.ds(g0, m)], rb.at[r_place, pl.ds(g0, m)], rss.at[ci], rrs.at[ci], to)
        for f in left_partners:
            to, c, _ = flipped(f)
            remote(ps.at[c, pl.ds(g0, m)], lb.at[place, pl.ds(g0, m)], lss.at[ci], lrs.at[ci], to)

        if ci > 0:
            part = plane_in(ci - 1)
            total[...] = part if ci == 1 else total[...] + part
    s_t = plane_in(NCH - 1)
    if NCH > 1:
        s_t = s_t + total[...]
    for r in range(8):
        at = 128 * (r // 3) + 40 * (r % 3)
        for q in range(3):
            st[q * 320 + r * 40 : q * 320 + r * 40 + 40, :] = s_t[at : at + 40, 128 * q : 128 * q + 128]

    lane8 = lanes_of((8, 128))

    for ci in range(NBC):
        l0, m = BACK[ci]
        for y in range(2):
            for l in range(l0, l0 + m):
                for q in range(3):
                    out = []
                    for h in range(2):
                        parts = [st[pl.ds(q * 320 + 160 * y + 10 * h + 3 * l + k, 8, stride=20), :] for k in range(3 if l < 3 else 1)]
                        per = []
                        for r in range(3 if q < 2 else 2):
                            moved = [pltpu.roll(v, (40 * (k - r)) % 128, 1) if k != r else v for k, v in enumerate(parts)]
                            moved += [jnp.zeros((8, 128), F32)] * (3 - len(moved))
                            per.append(jnp.where(lane8 < 40, moved[0], jnp.where(lane8 < 80, moved[1], moved[2])))
                        out.append(per)
                    for r in range(len(out[0])):
                        tiles[(3 * q + r) * 2 + y, l] = jnp.concatenate([out[0][r], out[1][r]], axis=0).astype(BF16)

        for f in left_partners:
            to, _, p = flipped(f)
            remote(tiles.at[p, pl.ds(l0, m)], back.at[channel * 2 + yh, pl.ds(l0, m)], ess.at[ci], ers.at[ci], to)
        back[channel * 2 + yh, pl.ds(l0, m)] = tiles[place, pl.ds(l0, m)]

    for ci, (l0, m) in enumerate(BACK):
        all_of(back.at[pl.ds(0, 15), pl.ds(l0, m)], ers.at[ci])

        @pl.loop(l0, l0 + m)
        def _(l):
            for h in range(2):
                for c in range(8):
                    tb[16 * c : 16 * c + 16, :] = back[c * 2 + h, l].astype(F32)
                for k in range(8):
                    rows = [tb[pl.ds(8 * u + k, 8, stride=16), :] for u in range(2)]
                    zb[8 * (k // 4) + 4 * h + k % 4, l] = jnp.concatenate(rows, axis=0).astype(BF16)

        for d in far_first:
            t, to = along(d)
            remote(zb.at[t, pl.ds(l0, m)], zo.at[z, pl.ds(l0, m)], bss.at[ci], brs.at[ci], to)
        zo[z, pl.ds(l0, m)] = zb[z, pl.ds(l0, m)]

    for l in range(NL):
        for ci, (l0, m) in enumerate(BACK):
            if l == l0:
                all_of(zo.at[pl.ds(0, 15), pl.ds(l0, m)], brs.at[ci])
        for h in range(2):
            v = jnp.concatenate([zo[t, l].astype(F32)[8 * h : 8 * h + 8] for t in range(NZ)], axis=0)
            center = jnp.mean(v, axis=0, keepdims=True)
            shifted = v - center
            spread = jnp.mean(shifted * shifted, axis=0, keepdims=True)
            x = (shifted * lax.rsqrt(spread + EPS) * gcol[...]).astype(BF16)
            u = lax.dot_general(x, outw_ref[...], tn, preferred_element_type=F32)
            for k in range(3 if l < 3 else 1):
                j = 10 * h + 3 * l + k
                at = 128 * (j // 3) + 40 * (j % 3)
                out_ref[j] = (pair_ref[j].astype(F32) + gat[at : at + 40, :] * u[40 * k : 40 * k + 40]).astype(BF16)

    for ci, (g0, m) in enumerate(CHUNKS):
        for ref, n, sem in ((zs, 15, zss), (ps, 15, lss), (ps, 7, rss), (rb, 8, fss)):
            all_of(ref.at[pl.ds(0, n), pl.ds(g0, m)], sem.at[ci])
    for ci, (l0, m) in enumerate(BACK):
        for ref, sem in ((tiles, ess), (zb, bss)):
            all_of(ref.at[pl.ds(0, 15), pl.ds(l0, m)], sem.at[ci])


def shards(pair, norm_gain, proj_weight, gate_weight, out_gain, out_weight):
    vm = pl.BlockSpec(memory_space=pltpu.VMEM)
    dma = pltpu.SemaphoreType.DMA
    out = pl.pallas_call(
        kernel,
        out_shape=jax.ShapeDtypeStruct((COLS, ROWS, 128), BF16),
        in_specs=[pl.BlockSpec(memory_space=pl.ANY)] * 6,
        out_specs=vm,
        scratch_shapes=[
            pltpu.VMEM((COLS, ROWS, 128), BF16),
            pltpu.VMEM((1, 128), F32),
            pltpu.VMEM((128, 512), BF16),
            pltpu.VMEM((128, 128), BF16),
            pltpu.VMEM((1, 128), F32),
            pltpu.VMEM((128, 128), BF16),
            pltpu.VMEM((NG * 128, 128), F32),
            pltpu.VMEM((NG * 128, 128), F32),
            pltpu.VMEM((512, 128), BF16),
            pltpu.VMEM((NZ, NG, 16, 128), BF16),
            pltpu.VMEM((NZ, NG, 16, 128), BF16),
            pltpu.VMEM((256, 128), F32),
            pltpu.VMEM((16, NG, 16, 128), BF16),
            pltpu.VMEM((16, NG, 16, 128), BF16),
            pltpu.VMEM((16, NG, 16, 128), BF16),
            pltpu.VMEM((KROWS, 384), BF16),
            pltpu.VMEM((KROWS, 384), BF16),
            pltpu.VMEM((384, 384), F32),
            pltpu.VMEM((960, 128), F32),
            pltpu.VMEM((16, NL, 16, 128), BF16),
            pltpu.VMEM((16, NL, 16, 128), BF16),
            pltpu.VMEM((NZ, NL, 16, 128), BF16),
            pltpu.VMEM((NZ, NL, 16, 128), BF16),
            pltpu.VMEM((128, 128), F32),
            dma((NCH,)), dma((NCH,)), dma((NCH,)), dma((NCH,)), dma((NCH,)), dma((NCH,)), dma((NCH,)), dma((NCH,)),
            dma((NBC,)), dma((NBC,)), dma((NBC,)), dma((NBC,)), dma((6,)),
        ],
        compiler_params=pltpu.CompilerParams(collective_id=0, has_side_effects=True, vmem_limit_bytes=63 * 1024 * 1024),
        name="triangle",
    )(jnp.transpose(pair, (1, 0, 2)), norm_gain.reshape(1, -1), proj_weight, gate_weight, out_gain.reshape(1, -1), out_weight)
    return jnp.transpose(out, (1, 0, 2))


def solution(mesh):
    in_specs = (P("row", "col", None), P(), P(), P(), P(), P())
    return jax.shard_map(shards, mesh=mesh, in_specs=in_specs, out_specs=P("row", "col", None), check_vma=False)
```

```python
import jax
import jax.numpy as jnp
from jax import lax
from jax.experimental import pallas as pl
from jax.experimental.pallas import tpu as pltpu
from jax.sharding import PartitionSpec as P

MESH = pl.DeviceIdType.MESH
F32 = jnp.float32
BF16 = jnp.bfloat16
EPS = 1e-05
NZ = 16
ROWS = 40
COLS = 20
NG = 7
CHUNKS = ((0, 4), (4, 3))
NCH = len(CHUNKS)
KROWS = 2 * 3 * NG * NZ
NL = 4
BACK = ((0, 1), (1, 3))
NBC = len(BACK)


def lanes_of(shape):
    return lax.broadcasted_iota(jnp.int32, shape, 1)


def rows_of(shape):
    return lax.broadcasted_iota(jnp.int32, shape, 0)


def kernel(pair_in, ngain_in, proj_in, gatew_in, ogain_in, outw_in, out_hbm,
           pair_ref, ngain_ref, proj_ref, gatew_ref, ogain_ref, outw_ref, out_ref, nf, gat, wt, zs, zr, tb, ps, lb, rb, lt, rt_, total, st, tiles, back, zb, zo, gcol,
           zss, zrs, lss, lrs, rss, rrs, fss, frs, ess, ers, bss, brs, ins, outs):
    row = lax.axis_index("row")
    col = lax.axis_index("col")
    z, yl = col % NZ, col // NZ
    x1, x0, yh, core = row // 8, (row // 4) % 2, (row // 2) % 2, row % 2

    fx1, fx0, fyh, fyl = 1 - 2 * x1, 1 - 2 * x0, 1 - 2 * yh, 1 - 2 * yl
    flips = {"x1": (8 * fx1, 0, 4 * fx1, 8 * fx1), "x0": (4 * fx0, 0, 2 * fx0, 4 * fx0),
             "yh": (2 * fyh, 0, 0, 2 * fyh), "yl": (0, NZ * fyl, fyl, fyl)}
    channel = x1 * 4 + x0 * 2 + yl
    place = (x1 * 4 + x0 * 2 + yh) * 2 + yl
    r_place = core * 8 + (x1 * 2 + x0) * 2 + yl
    sibling = {"row": row + 1 - 2 * core, "col": col}

    def flipped(names):
        r, c, k, p = row, col, channel, place
        for name in names:
            r, c, k, p = r + flips[name][0], c + flips[name][1], k + flips[name][2], p + flips[name][3]
        return {"row": r, "col": c}, k, p

    def subsets(names):
        found = [[n for i, n in enumerate(names) if m >> i & 1] for m in range(1, 2 ** len(names))]
        return sorted(found, key=lambda f: -len(f))

    left_partners = subsets(("x1", "x0", "yh", "yl"))
    right_partners = subsets(("x1", "x0", "yl"))
    far_first = [8] + [d for k in range(7, 0, -1) for d in (k, NZ - k)]

    def along(d):
        t = lax.rem(z + d, NZ)
        return t, {"row": row, "col": yl * NZ + t}

    def remote(src, dst, send_sem, recv_sem, to):
        pltpu.make_async_remote_copy(
            src_ref=src, dst_ref=dst, send_sem=send_sem, recv_sem=recv_sem, device_id=to, device_id_type=MESH).start()

    def all_of(ref, sem):
        pltpu.make_async_copy(ref, ref, sem).wait()

    ins_from = (pair_in, proj_in, ngain_in, gatew_in, ogain_in, outw_in)
    ins_to = (pair_ref, proj_ref, ngain_ref, gatew_ref, ogain_ref, outw_ref)
    fetch = [pltpu.make_async_copy(a, b, ins.at[n]) for n, (a, b) in enumerate(zip(ins_from, ins_to))]
    for f in fetch:
        f.start()

    barrier = pltpu.get_barrier_semaphore()
    greeted = [along(d)[1] for d in far_first]
    greeted += [flipped(f)[0] for f in left_partners] + [sibling]
    for to in greeted:
        pl.semaphore_signal(barrier, inc=1, device_id=to, device_id_type=MESH)

    nt = (((1,), (1,)), ((), ()))
    for ci, (g0, m) in enumerate(CHUNKS):
        if ci == 0:
            fetch[0].wait()
            fetch[2].wait()
        ngain = ngain_ref[...]
        for g in range(g0, g0 + m):
            for s in range(3):
                at = 128 * g + 40 * s
                if 3 * g + s < COLS:
                    v = pair_ref[3 * g + s].astype(F32)
                    center = jnp.mean(v, axis=-1, keepdims=True)
                    shifted = v - center
                    spread = jnp.mean(shifted * shifted, axis=-1, keepdims=True)
                    nf[at : at + 40, :] = shifted * lax.rsqrt(spread + EPS) * ngain
                else:
                    nf[at : at + 40, :] = jnp.zeros((40, 128), F32)
            nf[128 * g + 120 : 128 * g + 128, :] = jnp.zeros((8, 128), F32)
        if ci == 0:
            fetch[1].wait()
            wt[...] = proj_ref[...].astype(F32).T.astype(BF16)

        @pl.loop(g0, g0 + m)
        def _(g):
            n_g = nf[pl.ds(pl.multiple_of(g * 128, 128), 128), :].astype(BF16)
            p = lax.dot_general(wt[...], n_g, nt, preferred_element_type=F32)
            left = jax.nn.sigmoid(p[0:128]) * p[128:256]
            right = jax.nn.sigmoid(p[256:384]) * p[384:512]
            for t in range(NZ):
                zs[t, g] = jnp.concatenate([left[8 * t : 8 * t + 8], right[8 * t : 8 * t + 8]], axis=0).astype(BF16)

        if ci == 0:
            pl.semaphore_wait(barrier, len(greeted))

        for d in far_first:
            t, to = along(d)
            remote(zs.at[t, pl.ds(g0, m)], zr.at[z, pl.ds(g0, m)], zss.at[ci], zrs.at[ci], to)

    zr[z] = zs[z]

    for n in (3, 4, 5):
        fetch[n].wait()
    @pl.loop(0, NG)
    def _(g):
        rows = pl.ds(pl.multiple_of(g * 128, 128), 128)
        gat[rows, :] = jax.nn.sigmoid(jnp.dot(nf[rows, :].astype(BF16), gatew_ref[...], preferred_element_type=F32))

    gcol[...] = jnp.broadcast_to(ogain_ref[...], (128, 128)).T

    lane = lanes_of((NZ, 128))

    def regroup(src, dst, g, at):
        for y in range(2):
            for q in range(3):
                parts = [src[at(3 * q + s) + y, g].astype(F32) for s in range(3 if q < 2 else 2)]
                for k in range(3):
                    moved = [pltpu.roll(v, (40 * (s - k)) % 128, 1) if s != k else v for s, v in enumerate(parts)]
                    tile = jnp.where(lane < 40, moved[0], moved[1])
                    if len(moved) > 2:
                        tile = jnp.where(lane < 80, tile, moved[2])
                    dst[pl.ds(pl.multiple_of(((g * 2 + y) * 3 + k) * NZ, NZ), NZ), q * 128 : q * 128 + 128] = tile.astype(BF16)

    tn = (((0,), (0,)), ((), ()))

    def plane_in(ci):
        g0, m = CHUNKS[ci]
        all_of(rb.at[pl.ds(0, 7), pl.ds(g0, m)], rrs.at[ci])
        mine = rb.at[pl.ds(8 * core, 8), pl.ds(g0, m)]
        remote(mine, mine, fss.at[ci], frs.at[ci], sibling)
        all_of(lb.at[pl.ds(0, 15), pl.ds(g0, m)], lrs.at[ci])

        @pl.loop(g0, g0 + m)
        def _(g):
            regroup(lb, lt, g, lambda i: 2 * i)

        all_of(rb.at[pl.ds(0, 8), pl.ds(g0, m)], frs.at[ci])

        @pl.loop(g0, g0 + m)
        def _(g):
            regroup(rb, rt_, g, lambda j: 8 * (j % 2) + 2 * (j // 2))

        rows = pl.ds(g0 * 96, m * 96)
        return lax.dot_general(rt_[rows, :], lt[rows, :], tn, preferred_element_type=F32)

    for ci, (g0, m) in enumerate(CHUNKS):
        all_of(zr.at[pl.ds(0, 15), pl.ds(g0, m)], zrs.at[ci])

        @pl.loop(g0, g0 + m)
        def _(g):
            for t in range(NZ):
                tb[16 * t : 16 * t + 16, :] = zr[t, g].astype(F32)
            for c in range(16):
                ps[c, g] = tb[pl.ds(c, NZ, stride=16), :].astype(BF16)

        rb[r_place, pl.ds(g0, m)] = ps[8 + channel, pl.ds(g0, m)]
        lb[place, pl.ds(g0, m)] = ps[channel, pl.ds(g0, m)]
        for f in right_partners:
            to, c, _ = flipped(f)
            remote(ps.at[8 + c, pl.ds(g0, m)], rb.at[r_place, pl.ds(g0, m)], rss.at[ci], rrs.at[ci], to)
        for f in left_partners:
            to, c, _ = flipped(f)
            remote(ps.at[c, pl.ds(g0, m)], lb.at[place, pl.ds(g0, m)], lss.at[ci], lrs.at[ci], to)

        if ci > 0:
            part = plane_in(ci - 1)
            total[...] = part if ci == 1 else total[...] + part
    s_t = plane_in(NCH - 1)
    if NCH > 1:
        s_t = s_t + total[...]
    for r in range(8):
        at = 128 * (r // 3) + 40 * (r % 3)
        for q in range(3):
            st[q * 320 + r * 40 : q * 320 + r * 40 + 40, :] = s_t[at : at + 40, 128 * q : 128 * q + 128]

    lane8 = lanes_of((8, 128))

    for ci in range(NBC):
        l0, m = BACK[ci]
        for y in range(2):
            for l in range(l0, l0 + m):
                for q in range(3):
                    out = []
                    for h in range(2):
                        parts = [st[pl.ds(q * 320 + 160 * y + 10 * h + 3 * l + k, 8, stride=20), :] for k in range(3 if l < 3 else 1)]
                        per = []
                        for r in range(3 if q < 2 else 2):
                            moved = [pltpu.roll(v, (40 * (k - r)) % 128, 1) if k != r else v for k, v in enumerate(parts)]
                            moved += [jnp.zeros((8, 128), F32)] * (3 - len(moved))
                            per.append(jnp.where(lane8 < 40, moved[0], jnp.where(lane8 < 80, moved[1], moved[2])))
                        out.append(per)
                    for r in range(len(out[0])):
                        tiles[(3 * q + r) * 2 + y, l] = jnp.concatenate([out[0][r], out[1][r]], axis=0).astype(BF16)

        for f in left_partners:
            to, _, p = flipped(f)
            remote(tiles.at[p, pl.ds(l0, m)], back.at[channel * 2 + yh, pl.ds(l0, m)], ess.at[ci], ers.at[ci], to)
        back[channel * 2 + yh, pl.ds(l0, m)] = tiles[place, pl.ds(l0, m)]

    for ci, (l0, m) in enumerate(BACK):
        all_of(back.at[pl.ds(0, 15), pl.ds(l0, m)], ers.at[ci])

        @pl.loop(l0, l0 + m)
        def _(l):
            for h in range(2):
                for c in range(8):
                    tb[16 * c : 16 * c + 16, :] = back[c * 2 + h, l].astype(F32)
                for k in range(8):
                    rows = [tb[pl.ds(8 * u + k, 8, stride=16), :] for u in range(2)]
                    zb[8 * (k // 4) + 4 * h + k % 4, l] = jnp.concatenate(rows, axis=0).astype(BF16)

        for d in far_first:
            t, to = along(d)
            remote(zb.at[t, pl.ds(l0, m)], zo.at[z, pl.ds(l0, m)], bss.at[ci], brs.at[ci], to)
        zo[z, pl.ds(l0, m)] = zb[z, pl.ds(l0, m)]

    leaving = []
    for l in range(NL):
        for ci, (l0, m) in enumerate(BACK):
            if l == l0:
                all_of(zo.at[pl.ds(0, 15), pl.ds(l0, m)], brs.at[ci])
        for h in range(2):
            v = jnp.concatenate([zo[t, l].astype(F32)[8 * h : 8 * h + 8] for t in range(NZ)], axis=0)
            center = jnp.mean(v, axis=0, keepdims=True)
            shifted = v - center
            spread = jnp.mean(shifted * shifted, axis=0, keepdims=True)
            x = (shifted * lax.rsqrt(spread + EPS) * gcol[...]).astype(BF16)
            u = lax.dot_general(x, outw_ref[...], tn, preferred_element_type=F32)
            for k in range(3 if l < 3 else 1):
                j = 10 * h + 3 * l + k
                at = 128 * (j // 3) + 40 * (j % 3)
                out_ref[j] = (pair_ref[j].astype(F32) + gat[at : at + 40, :] * u[40 * k : 40 * k + 40]).astype(BF16)

            j0, n = 10 * h + 3 * l, 3 if l < 3 else 1
            leaving.append(pltpu.make_async_copy(out_ref.at[pl.ds(j0, n)], out_hbm.at[pl.ds(j0, n)], outs.at[2 * l + h]))
            leaving[-1].start()

    for ci, (g0, m) in enumerate(CHUNKS):
        for ref, n, sem in ((zs, 15, zss), (ps, 15, lss), (ps, 7, rss), (rb, 8, fss)):
            all_of(ref.at[pl.ds(0, n), pl.ds(g0, m)], sem.at[ci])
    for ci, (l0, m) in enumerate(BACK):
        for ref, sem in ((tiles, ess), (zb, bss)):
            all_of(ref.at[pl.ds(0, 15), pl.ds(l0, m)], sem.at[ci])
    for part in leaving:
        part.wait()


def shards(pair, norm_gain, proj_weight, gate_weight, out_gain, out_weight):
    dma = pltpu.SemaphoreType.DMA
    out = pl.pallas_call(
        kernel,
        out_shape=jax.ShapeDtypeStruct((COLS, ROWS, 128), BF16),
        in_specs=[pl.BlockSpec(memory_space=pl.ANY)] * 6,
        out_specs=pl.BlockSpec(memory_space=pl.ANY),
        scratch_shapes=[
            pltpu.VMEM((COLS, ROWS, 128), BF16),
            pltpu.VMEM((1, 128), F32),
            pltpu.VMEM((128, 512), BF16),
            pltpu.VMEM((128, 128), BF16),
            pltpu.VMEM((1, 128), F32),
            pltpu.VMEM((128, 128), BF16),
            pltpu.VMEM((COLS, ROWS, 128), BF16),
            pltpu.VMEM((NG * 128, 128), F32),
            pltpu.VMEM((NG * 128, 128), F32),
            pltpu.VMEM((512, 128), BF16),
            pltpu.VMEM((NZ, NG, 16, 128), BF16),
            pltpu.VMEM((NZ, NG, 16, 128), BF16),
            pltpu.VMEM((256, 128), F32),
            pltpu.VMEM((16, NG, 16, 128), BF16),
            pltpu.VMEM((16, NG, 16, 128), BF16),
            pltpu.VMEM((16, NG, 16, 128), BF16),
            pltpu.VMEM((KROWS, 384), BF16),
            pltpu.VMEM((KROWS, 384), BF16),
            pltpu.VMEM((384, 384), F32),
            pltpu.VMEM((960, 128), F32),
            pltpu.VMEM((16, NL, 16, 128), BF16),
            pltpu.VMEM((16, NL, 16, 128), BF16),
            pltpu.VMEM((NZ, NL, 16, 128), BF16),
            pltpu.VMEM((NZ, NL, 16, 128), BF16),
            pltpu.VMEM((128, 128), F32),
            dma((NCH,)), dma((NCH,)), dma((NCH,)), dma((NCH,)), dma((NCH,)), dma((NCH,)), dma((NCH,)), dma((NCH,)),
            dma((NBC,)), dma((NBC,)), dma((NBC,)), dma((NBC,)), dma((6,)), dma((2 * NL,)),
        ],
        compiler_params=pltpu.CompilerParams(collective_id=0, has_side_effects=True, vmem_limit_bytes=63 * 1024 * 1024),
        name="triangle",
    )(jnp.transpose(pair, (1, 0, 2)), norm_gain.reshape(1, -1), proj_weight, gate_weight, out_gain.reshape(1, -1), out_weight)
    return jnp.transpose(out, (1, 0, 2))


def solution(mesh):
    in_specs = (P("row", "col", None), P(), P(), P(), P(), P())
    return jax.shard_map(shards, mesh=mesh, in_specs=in_specs, out_specs=P("row", "col", None), check_vma=False)
```
